512 devices in a mesh: gx: 8 (over x, core), gz: 64 (over z, y).
Axes of the slice: x: 4, y: 4, z: 16, core: 2. Of those that a mesh axis runs over, the one named last changes fastest.
Arguments:
- adjoint: float32 [4, 32, 512, 768], P(None, 'gx', 'gz'), may hold values from -6 to 6
- mean_velocity: float32 [512], P('gz'), may hold values from 0.2 to 1.5
- mean_shear: float32 [512], P('gz'), may hold values from -1 to 3
- viscous_inverse: float32 [512, 512], replicated
- sensor_rows: float32 [8, 64, 64, 8, 128], P('gx', 'gz'), may hold values from -6 to 6
- sensor_cells: int32 [8, 64, 64, 8], P('gx', 'gz'), may hold values from 0 to 47
- sensor_counts: int32 [8, 64, 64], P('gx', 'gz'), may hold values from 0 to 8, as said below
Outputs:
- updated: float32 [4, 32, 512, 768], P(None, 'gx', 'gz')
The draws below stay inside these ranges and needn't reach their ends.
Inputs may be any that keep to these rules, and one draw needn't show every extreme that they name: `sensor_counts`: slots at or beyond the count are ignored. In every slab some owner receives 8 rows from every device. `sensor_cells`: entries of slots that are not used carry no meaning.
All inputs are finite; a program needn't handle non-finite values.
Results may differ from the reference program's by a relative error of at most 0.00007.
Values sent between devices are 32-bit elements; how exact they have to be, the bound alone decides.
A program may use at most 64 MiB of HBM per device.

```python
import jax
import jax.numpy as jnp
from jax import lax

F = 4
NY = 512
KW = 32
XL = 4
ZL = 12
CAP = 8
ROW = 128
SLABS = 8
OWNERS = 64
NX = 32
NZ = 768


def draw_viscous_inverse(key, part):
    key = jax.random.fold_in(key, 7)
    key_diag, key_off = jax.random.split(key)
    diagonal = jax.random.uniform(key_diag, (NY,), jnp.float32, 0.8, 1.6)
    off = jax.random.normal(key_off, (NY, NY), jnp.float32) * (0.6 / NY ** 0.5)
    levels = jnp.arange(NY, dtype=jnp.int32)
    identity = (levels[:, None] == levels[None, :]).astype(jnp.float32)
    return off + identity * diagonal[:, None]


def draw_sensor_counts(key, part):
    key = jax.random.fold_in(key, 11)
    key_base, key_hot = jax.random.split(key)
    base = jax.random.randint(key_base, (SLABS, OWNERS, OWNERS), 0, CAP * 3 // 4 + 1, dtype=jnp.int32)
    offset = jax.random.randint(key_hot, (SLABS, 1, 1), 0, OWNERS, dtype=jnp.int32)
    owner = jnp.arange(OWNERS, dtype=jnp.int32)[None, None, :]
    hot_count = max(1, OWNERS // 16)
    hot = (owner - offset) % OWNERS < hot_count
    return jnp.where(hot, CAP, base).astype(jnp.int32)


def with_ends(entries, rng, least, high):
    spot = [jax.random.randint(jax.random.fold_in(rng, axis), (), 0, length) for axis, length in enumerate(entries.shape)]
    longest = entries.shape.index(max(entries.shape))
    next_to = spot[:longest] + [(spot[longest] + 1) % entries.shape[longest]] + spot[longest + 1:]
    return entries.at[tuple(spot)].set(least).at[tuple(next_to)].set(high)


def level_of(rng, extent, cuts, low, high):
    loudness = 1.0
    for axis_at, shards_of in cuts:
        steps = jax.random.uniform(jax.random.fold_in(jax.random.fold_in(rng, 6), axis_at), (shards_of,), jnp.float32, low / len(cuts), high / len(cuts))
        loudness = loudness * jnp.repeat(jnp.exp(steps), extent[axis_at] // shards_of).reshape((-1,) + (1,) * (len(extent) - 1 - axis_at))
    return loudness


def gaussian(own_key, shape, deviation, reach, cuts=(), kind=jnp.bfloat16):
    result = deviation * jax.random.normal(own_key, shape, jnp.float32)
    if cuts:
        result = result * level_of(own_key, shape, cuts, -0.22, 0.18)
    return jnp.clip(result, -reach, reach).astype(kind)


def setup_inputs(seed: int = 0) -> dict:
    streams_of = jax.random.split(jax.random.key(seed), 8)
    adjoint = gaussian(streams_of[0], (F, NX, NY, NZ), 1.0, 6.0, ((1, 8), (2, 64)), jnp.float32)
    mean_velocity = jnp.clip(0.2 + 1.3 * jax.random.uniform(streams_of[1], (NY,), jnp.float32) ** level_of(streams_of[1], (NY,), ((0, 64),), -0.2, 0.2), 0.2, 1.5)
    mean_shear = jnp.clip(-1.0 + 4.0 * jax.random.uniform(streams_of[2], (NY,), jnp.float32) ** level_of(streams_of[2], (NY,), ((0, 64),), -0.2, 0.2), -1.0, 3.0)
    viscous_inverse = draw_viscous_inverse(jax.random.fold_in(streams_of[7], 71), 0)
    sensor_rows = gaussian(streams_of[4], (SLABS, OWNERS, OWNERS, CAP, ROW), 1.0, 6.0, ((0, 8), (1, 64)), jnp.float32)
    sensor_cells = with_ends(jax.random.randint(streams_of[5], (SLABS, OWNERS, OWNERS, CAP), 0, XL * ZL), jax.random.fold_in(streams_of[5], 1), 0, (XL * ZL) - 1).astype(jnp.int32)
    sensor_counts = draw_sensor_counts(jax.random.fold_in(streams_of[7], 71), 0)
    return {"adjoint": adjoint, "mean_velocity": mean_velocity, "mean_shear": mean_shear, "viscous_inverse": viscous_inverse, "sensor_rows": sensor_rows, "sensor_cells": sensor_cells, "sensor_counts": sensor_counts}


def reference(adjoint, mean_velocity, mean_shear, viscous_inverse, sensor_rows, sensor_cells, sensor_counts):
    streamwise = (jnp.roll(adjoint, -1, axis=1) - jnp.roll(adjoint, 1, axis=1)) / 2.0
    spanwise = jnp.roll(adjoint, -1, axis=3) + jnp.roll(adjoint, 1, axis=3) - 2.0 * adjoint
    explicit = adjoint + 0.5 * mean_velocity[None, None, :, None] * streamwise + 0.25 * spanwise
    explicit = explicit.at[1].add(0.5 * mean_shear[None, :, None] * adjoint[0])
    slots = jnp.arange(CAP, dtype=jnp.int32)
    usable = (slots[None, None, None, :] < sensor_counts[..., None]).astype(jnp.float32)
    slab_index = jnp.arange(SLABS, dtype=jnp.int32)[:, None, None, None]
    owner_index = jnp.arange(OWNERS, dtype=jnp.int32)[None, None, :, None]
    x_cell = (slab_index * XL + sensor_cells // ZL).astype(jnp.int32)
    z_cell = (owner_index * ZL + sensor_cells % ZL).astype(jnp.int32)
    masked = sensor_rows * usable[..., None]
    wall = jnp.zeros((NX, NZ, ROW), jnp.float32).at[x_cell, z_cell].add(masked)
    wall = wall.reshape(NX, NZ, F, KW).transpose(2, 0, 3, 1)
    forced = explicit.at[:, :, :KW, :].add(wall)
    return jnp.einsum("fxkz,yk->fxyz", forced, viscous_inverse, precision=lax.Precision.HIGHEST)
```

```python
import functools

import jax
import jax.numpy as jnp
from jax import lax
from jax.experimental import pallas as pl
from jax.experimental.pallas import tpu as pltpu
from jax.sharding import PartitionSpec as P

MESH = pl.DeviceIdType.MESH
BF16 = jnp.bfloat16
F32 = jnp.float32

F, XL, NZ, NY = 4, 4, 768, 512
LEV = 8
NGX, NGZ, GY, GZ = 8, 64, 4, 16
WIN = NZ // GZ
ZL = 12
CAP = 8
KW = 32
ROWS = 12


def iota(shape, dim):
    return lax.broadcasted_iota(jnp.int32, shape, dim)


def split(x):
    hi = x.astype(BF16)
    return hi, (x - hi.astype(F32)).astype(BF16)


def dot(a, b):
    return jnp.dot(a, b, preferred_element_type=F32)


def pack(e, w):
    at = WIN * w
    first = jnp.concatenate(
        [e[0][:, at : at + 48], e[1][:, at : at + 48], e[2][:, at : at + 32]], axis=1
    )
    second = jnp.concatenate([e[2][:, at + 32 : at + 48], e[3][:, at : at + 48]], axis=1)
    return first, jnp.concatenate([second[0:4], second[4:8]], axis=1)


def kernel(
    adj_hbm, vel_ref, shear_ref, m_hbm, rows_hbm, cells_hbm, counts_hbm,
    out_ref,
    adj, halo, m_f32, mh, ml, cells, counts, wsend, wrecv, fsend, frecv, bsend, brecv, xsend, xrecv,
    local_sem, halo_send, halo_recv, w_send, w_recv, f_send, f_recv, b_send, b_recv, x_send, x_recv,
):
    gx = lax.axis_index("gx")
    me = lax.axis_index("gz")
    z = me // GY
    y = lax.rem(me, GY)

    def remote(src, dst, ss, rs, ix, iz):
        return pltpu.make_async_remote_copy(
            src_ref=src, dst_ref=dst, send_sem=ss, recv_sem=rs, device_id=(ix, iz), device_id_type=MESH
        )

    barrier = pltpu.get_barrier_semaphore()
    after, before = lax.rem(gx + 1, NGX), lax.rem(gx + NGX - 1, NGX)
    for ix in (after, before):
        pl.semaphore_signal(barrier, inc=1, device_id=(ix, me), device_id_type=MESH)

    def greet(i, c):
        pl.semaphore_signal(
            barrier, inc=1, device_id=(gx, lax.rem(me + i, NGZ)), device_id_type=MESH
        )
        return c

    lax.fori_loop(1, NGZ, greet, 0)

    loads = [
        pltpu.make_async_copy(adj_hbm, adj, local_sem.at[0]),
        pltpu.make_async_copy(cells_hbm.at[0, 0], cells, local_sem.at[1]),
        pltpu.make_async_copy(counts_hbm.at[0], counts, local_sem.at[2]),
        pltpu.make_async_copy(rows_hbm.at[0, 0], wsend.at[:, pl.ds(0, CAP)], local_sem.at[3]),
        pltpu.make_async_copy(m_hbm, m_f32, local_sem.at[4]),
    ]
    for load in loads:
        load.start()

    loads[1].wait()
    loads[2].wait()
    counts_row = jnp.broadcast_to(counts[...].astype(F32), (NGZ, NGZ))
    diagonal = iota((NGZ, NGZ), 0) == iota((NGZ, NGZ), 1)
    counts_col = jnp.sum(jnp.where(diagonal, counts_row, 0.0), axis=1, keepdims=True)
    slot = iota((NGZ, CAP), 1).astype(F32)
    used_cells = jnp.where(slot < counts_col, cells[...].astype(F32), -1.0)
    loads[3].wait()
    wsend[:, CAP, :] = jnp.concatenate(
        [used_cells, jnp.zeros((NGZ, 128 - CAP), F32)], axis=1
    )

    level = iota((LEV, NZ), 0)
    velocity = jnp.zeros((LEV, NZ), F32)
    shear = jnp.zeros((LEV, NZ), F32)
    for i in range(LEV):
        velocity = jnp.where(level == i, vel_ref[i], velocity)
        shear = jnp.where(level == i, shear_ref[i], shear)

    def step_and_pack(x):
        rows = []
        for f in range(F):
            here = adj[f, x]
            up = adj[f, x + 1] if x < XL - 1 else halo[1, f]
            down = adj[f, x - 1] if x > 0 else halo[0, f]
            spanwise = pltpu.roll(here, NZ - 1, 1) + pltpu.roll(here, 1, 1) - 2.0 * here
            e = here + 0.5 * velocity * ((up - down) / 2.0) + 0.25 * spanwise
            if f == 1:
                e = e + 0.5 * shear * adj[0, x]
            rows.append(e)
        for w in range(GZ):
            first, second = pack(rows, w)
            fsend[w * GY + x, 0:8, :] = first
            fsend[w * GY + x, 8:12, :] = second

    loads[0].wait()
    step_and_pack(1)
    step_and_pack(2)

    pl.semaphore_wait(barrier, NGZ - 1 + 2)

    halos = [
        remote(adj.at[:, XL - 1], halo.at[0], halo_send.at[0], halo_recv.at[0], after, me),
        remote(adj.at[:, 0], halo.at[1], halo_send.at[1], halo_recv.at[1], before, me),
    ]
    for h in halos:
        h.start()

    def send_wall(i, c):
        d = lax.rem(me + i, NGZ)
        remote(wsend.at[d], wrecv.at[me], w_send, w_recv, gx, d).start()
        return c

    lax.fori_loop(1, NGZ, send_wall, 0)
    wrecv[me] = wsend[me]

    def send_fields(first, second):
        def body(i, c):
            for x in (first, second):
                d = lax.rem(z + i, GZ) * GY + x

                @pl.when(d != me)
                def _():
                    remote(fsend.at[d], frecv.at[me], f_send, f_recv, gx, d).start()

            return c

        lax.fori_loop(0, GZ, body, 0)

    send_fields(1, 2)
    for h in halos:
        h.wait_recv()
    step_and_pack(0)
    step_and_pack(3)
    send_fields(0, 3)
    frecv[me] = fsend[me]

    loads[4].wait()
    m_hi, m_lo = split(m_f32[...])
    mh[...] = m_hi
    ml[...] = m_lo

    others = pl.ds(0, NGZ - 1)
    pltpu.make_async_copy(wsend.at[others], wrecv.at[others], w_recv).wait()
    slots = NGZ * CAP
    got = wrecv[:, CAP, :].astype(BF16)[:, 0:CAP]
    tile = (iota((CAP, slots), 0) == lax.rem(iota((CAP, slots), 1), CAP)).astype(BF16)
    spread = dot(got, tile)
    mine = iota((NGZ, slots), 0) == iota((NGZ, slots), 1) // CAP
    cell_row = jnp.sum(jnp.where(mine, spread, 0.0), axis=0, keepdims=True)
    place = iota((64, slots), 0)
    inside = lax.rem(place, 16) < ZL
    target = jnp.where(inside, (place // 16) * ZL + lax.rem(place, 16), -2).astype(F32)
    onehot = jnp.where(target == cell_row, 1.0, 0.0).astype(BF16)
    r_hi, r_lo = split(wrecv[:, 0:CAP, :].reshape(slots, 128))
    wall = dot(onehot, r_hi) + dot(onehot, r_lo)
    xsend[...] = wall.reshape(XL, 16, 128)
    for k in range(1, GY):
        other = lax.rem(y + k, GY)
        remote(
            xsend.at[other], xrecv.at[y], x_send.at[k - 1], x_recv.at[k - 1], gx, z * GY + other
        ).start()
    xrecv[y] = xsend[y]
    for k in range(1, GY):
        pltpu.make_async_copy(xsend.at[0], xrecv.at[0], x_recv.at[k - 1]).wait()
    wall_t = jnp.transpose(xrecv[...].reshape(64, 128))
    p = iota((64, 192), 0)
    col = iota((64, 192), 1)
    forcing = jnp.zeros((KW, 192), F32)
    for f in range(F):
        there = (lax.rem(p, 16) < ZL) & (col == WIN * f + ZL * (p // 16) + lax.rem(p, 16))
        there = jnp.where(there, 1.0, 0.0).astype(BF16)
        v_hi, v_lo = split(wall_t[KW * f : KW * (f + 1)])
        forcing = forcing + dot(v_hi, there) + dot(v_lo, there)

    pltpu.make_async_copy(fsend.at[others], frecv.at[others], f_recv).wait()
    left = frecv[:, 0:8, :].reshape(NY, 128)
    tail = frecv[:, 8:12, :]
    right = jnp.concatenate([tail[:, :, 0:64], tail[:, :, 64:128]], axis=1).reshape(NY, 64)
    columns = jnp.concatenate([left, right], axis=1)
    columns = jnp.concatenate([columns[0:KW] + forcing, columns[KW:]], axis=0)
    c_hi, c_lo = split(columns)
    solved = dot(mh[...], c_hi) + dot(mh[...], c_lo) + dot(ml[...], c_hi)
    bsend[:, 0:8, :] = solved[:, 0:128].reshape(NGZ, LEV, 128)
    back = solved[:, 128:192].reshape(NGZ, LEV, 64)
    bsend[:, 8:12, :] = jnp.concatenate([back[:, 0:4, :], back[:, 4:8, :]], axis=2)

    def send_back(i, c):
        d = lax.rem(me + i, NGZ)
        remote(bsend.at[d], brecv.at[me], b_send, b_recv, gx, d).start()
        return c

    lax.fori_loop(1, NGZ, send_back, 0)
    brecv[me] = bsend[me]
    pltpu.make_async_copy(bsend.at[others], brecv.at[others], b_recv).wait()

    for x in range(XL):
        pieces = [[] for _ in range(F)]
        for w in range(GZ):
            b0 = brecv[w * GY + x, 0:8, :]
            b1 = brecv[w * GY + x, 8:12, :]
            b1 = jnp.concatenate([b1[:, 0:64], b1[:, 64:128]], axis=0)
            pieces[0].append(b0[:, 0:48])
            pieces[1].append(b0[:, 48:96])
            pieces[2].append(b0[:, 96:128])
            pieces[2].append(b1[:, 0:16])
            pieces[3].append(b1[:, 16:64])
        for f in range(F):
            out_ref[f, x] = jnp.concatenate(pieces[f], axis=1)

    for h in halos:
        h.wait_send()
    pltpu.make_async_copy(wsend.at[others], wrecv.at[others], w_send).wait()
    pltpu.make_async_copy(fsend.at[others], frecv.at[others], f_send).wait()
    pltpu.make_async_copy(bsend.at[others], brecv.at[others], b_send).wait()
    for k in range(1, GY):
        pltpu.make_async_copy(xsend.at[0], xrecv.at[0], x_send.at[k - 1]).wait()


def on_device(adjoint, velocity, shear, matrix, rows, cells, counts):
    anywhere = pl.BlockSpec(memory_space=pl.ANY)
    smem = pl.BlockSpec(memory_space=pltpu.SMEM)
    vmem = pltpu.VMEM
    dma = pltpu.SemaphoreType.DMA
    message = vmem((NGZ, ROWS, 128), F32)
    return pl.pallas_call(
        kernel,
        out_shape=jax.ShapeDtypeStruct((F, XL, LEV, NZ), F32),
        in_specs=[anywhere, smem, smem, anywhere, anywhere, anywhere, anywhere],
        out_specs=pl.BlockSpec(memory_space=pltpu.VMEM),
        scratch_shapes=[
            vmem((F, XL, LEV, NZ), F32),
            vmem((2, F, LEV, NZ), F32),
            vmem((NY, NY), F32),
            vmem((NY, NY), BF16),
            vmem((NY, NY), BF16),
            vmem((NGZ, CAP), jnp.int32),
            vmem((1, NGZ), jnp.int32),
            vmem((NGZ, CAP + 1, 128), F32),
            vmem((NGZ, CAP + 1, 128), F32),
            message, message, message, message,
            vmem((GY, 16, 128), F32),
            vmem((GY, 16, 128), F32),
            dma((5,)), dma((2,)), dma((2,)), dma, dma, dma, dma, dma, dma, dma((3,)), dma((3,)),
        ],
        compiler_params=pltpu.CompilerParams(
            collective_id=0, has_side_effects=True, vmem_limit_bytes=48 * 1024 * 1024
        ),
        cost_estimate=pl.CostEstimate(flops=310_000_000, bytes_accessed=3_000_000, transcendentals=0),
    )(adjoint, velocity, shear, matrix, rows, cells, counts)


def solution(mesh):
    in_specs = (
        P(None, "gx", "gz", None),
        P("gz"),
        P("gz"),
        P(),
        P("gx", "gz", None, None, None),
        P("gx", "gz", None, None),
        P("gx", "gz", None),
    )
    return jax.shard_map(
        on_device, mesh=mesh, in_specs=in_specs, out_specs=P(None, "gx", "gz", None), check_vma=False
    )
```

```python
import functools

import jax
import jax.numpy as jnp
from jax import lax
from jax.experimental import pallas as pl
from jax.experimental.pallas import tpu as pltpu
from jax.sharding import PartitionSpec as P

MESH = pl.DeviceIdType.MESH
BF16 = jnp.bfloat16
F32 = jnp.float32

F, XL, NZ, NY = 4, 4, 768, 512
LEV = 8
NGX, NGZ, GY, GZ = 8, 64, 4, 16
WIN = NZ // GZ
ZL = 12
CAP = 8
KW = 32
NEAR = 4
DIRECT, RIGHT, LEFT = 0, 28, 46
ROWS = 12


def iota(shape, dim):
    return lax.broadcasted_iota(jnp.int32, shape, dim)


def split(x):
    hi = x.astype(BF16)
    return hi, (x - hi.astype(F32)).astype(BF16)


def dot(a, b):
    return jnp.dot(a, b, preferred_element_type=F32)


def pack(e, w):
    at = WIN * w
    first = jnp.concatenate(
        [e[0][:, at : at + 48], e[1][:, at : at + 48], e[2][:, at : at + 32]], axis=1
    )
    second = jnp.concatenate([e[2][:, at + 32 : at + 48], e[3][:, at : at + 48]], axis=1)
    return first, jnp.concatenate([second[0:4], second[4:8]], axis=1)


def kernel(
    adj_hbm, vel_ref, shear_ref, m_hbm, rows_hbm, cells_hbm, counts_hbm,
    out_ref,
    adj, halo, m_f32, mh, ml, cells, counts, wsend, wrecv, fsend, frecv, bsend, brecv, xsend, xrecv, dsend, drecv,
    local_sem, halo_send, halo_recv, w_send, w_recv, f_send, f_recv, b_send, b_recv, x_send, x_recv, d_send, d_recv, known,
):
    gx = lax.axis_index("gx")
    me = lax.axis_index("gz")
    z = me // GY
    y = lax.rem(me, GY)

    def remote(src, dst, ss, rs, ix, iz):
        return pltpu.make_async_remote_copy(
            src_ref=src, dst_ref=dst, send_sem=ss, recv_sem=rs, device_id=(ix, iz), device_id_type=MESH
        )

    def at(dz, iy):
        return lax.rem(z + dz + GZ, GZ) * GY + iy

    def signal(sem, ix, iz):
        pl.semaphore_signal(sem, inc=1, device_id=(ix, iz), device_id_type=MESH)

    barrier = pltpu.get_barrier_semaphore()
    after, before = lax.rem(gx + 1, NGX), lax.rem(gx + NGX - 1, NGX)
    signal(barrier, after, me)
    signal(barrier, before, me)

    def greet_here(k, c):
        signal(barrier, gx, at(0, lax.rem(y + k, GY)))
        return c

    def greet_near(k, c):
        signal(barrier, gx, at(NEAR - k // GY, lax.rem(k, GY)))
        signal(barrier, gx, at(k // GY - NEAR, lax.rem(k, GY)))
        return c

    lax.fori_loop(1, GY, greet_here, 0)
    lax.fori_loop(0, NEAR * GY, greet_near, 0)

    loads = [
        pltpu.make_async_copy(adj_hbm, adj, local_sem.at[0]),
        pltpu.make_async_copy(cells_hbm.at[0, 0], cells, local_sem.at[1]),
        pltpu.make_async_copy(counts_hbm.at[0], counts, local_sem.at[2]),
        pltpu.make_async_copy(rows_hbm.at[0, 0], wsend.at[:, pl.ds(0, CAP)], local_sem.at[3]),
        pltpu.make_async_copy(m_hbm, m_f32, local_sem.at[4]),
    ]
    for load in loads:
        load.start()

    loads[1].wait()
    loads[2].wait()
    used = iota((CAP, NGZ), 0) < counts[...]
    used_cells = jnp.where(used, cells[...], -1).astype(F32)
    used_cells = jnp.concatenate([used_cells, jnp.zeros((128 - CAP, NGZ), F32)], axis=0)
    loads[3].wait()
    wsend[:, CAP, :] = jnp.transpose(used_cells)

    level = iota((LEV, NZ), 0)
    velocity = jnp.zeros((LEV, NZ), F32)
    shear = jnp.zeros((LEV, NZ), F32)
    for i in range(LEV):
        velocity = jnp.where(level == i, vel_ref[i], velocity)
        shear = jnp.where(level == i, shear_ref[i], shear)

    def step_and_pack(x):
        rows = []
        for f in range(F):
            here = adj[f, x]
            up = adj[f, x + 1] if x < XL - 1 else halo[1, f]
            down = adj[f, x - 1] if x > 0 else halo[0, f]
            spanwise = pltpu.roll(here, NZ - 1, 1) + pltpu.roll(here, 1, 1) - 2.0 * here
            e = here + 0.5 * velocity * ((up - down) / 2.0) + 0.25 * spanwise
            if f == 1:
                e = e + 0.5 * shear * adj[0, x]
            rows.append(e)
        for w in range(GZ):
            first, second = pack(rows, w)
            fsend[w * GY + x, 0:8, :] = first
            fsend[w * GY + x, 8:12, :] = second

    loads[0].wait()
    step_and_pack(1)
    step_and_pack(2)

    pl.semaphore_wait(barrier, 2 + (GY - 1) + 2 * NEAR * GY)
    signal(known, gx, at(NEAR, y))
    signal(known, gx, at(-NEAR, y))

    halos = [
        remote(adj.at[:, XL - 1], halo.at[0], halo_send.at[0], halo_recv.at[0], after, me),
        remote(adj.at[:, 0], halo.at[1], halo_send.at[1], halo_recv.at[1], before, me),
    ]
    for h in halos:
        h.start()

    def send_wall(owner_dz, dz, iy, slot):
        owner, dest = at(owner_dz, iy), at(dz, iy)
        remote(wsend.at[owner], wrecv.at[slot], w_send, w_recv, gx, dest).start()

    def send_field(dz, x):
        dest = at(dz, x)
        remote(fsend.at[dest], frecv.at[me], f_send, f_recv, gx, dest).start()

    def wall_here(k, c):
        iy = lax.rem(y + k, GY)
        send_wall(0, 0, iy, DIRECT + 3 * GY + y)
        send_wall(4, 0, iy, RIGHT + y)
        send_wall(-4, 0, iy, LEFT + y)
        return c

    lax.fori_loop(1, GY, wall_here, 0)
    wrecv[DIRECT + 3 * GY + y] = wsend[me]
    wrecv[RIGHT + y] = wsend[at(4, y)]
    wrecv[LEFT + y] = wsend[at(-4, y)]

    def wall_at(level):
        def body(iy, c):
            send_wall(level, level, iy, DIRECT + (3 + level) * GY + y)
            send_wall(-level, -level, iy, DIRECT + (3 - level) * GY + y)
            send_wall(4 + level, level, iy, RIGHT + level * GY + y)
            send_wall(-4 - level, -level, iy, LEFT + level * GY + y)
            return c

        lax.fori_loop(0, GY, body, 0)

    for level in (1, 2, 3):
        wall_at(level)
    odd = lax.rem(y, 2)
    dz8 = NEAR - 2 * NEAR * odd
    slot8 = jnp.where(odd == 1, LEFT, RIGHT) + 4 * GY + y // 2

    def wall_8(iy, c):
        send_wall(8, dz8, iy, slot8)
        return c

    lax.fori_loop(0, GY, wall_8, 0)

    def fields_at(first, last, xs):
        def body(level, c):
            for x in xs:
                send_field(level, x)
                send_field(-level, x)
            return c

        lax.fori_loop(first, last, body, 0)

    def fields_here(xs):
        for x in xs:

            @pl.when(x != y)
            def _():
                send_field(0, x)

    fields_at(1, NEAR + 1, (1, 2))
    fields_here((1, 2))
    for h in halos:
        h.wait_recv()
    step_and_pack(0)
    step_and_pack(3)
    fields_at(1, NEAR + 1, (0, 3))
    fields_here((0, 3))
    frecv[me] = fsend[me]

    others = pl.ds(0, NGZ - 1)
    got_wall = pl.ds(0, NGZ - 3)
    pltpu.make_async_copy(wsend.at[got_wall], wrecv.at[got_wall], w_recv).wait()
    slots = NGZ * CAP
    got = wrecv[:, CAP, :].astype(BF16)[:, 0:CAP]
    tile = (iota((CAP, slots), 0) == lax.rem(iota((CAP, slots), 1), CAP)).astype(BF16)
    spread = dot(got, tile)
    mine = iota((NGZ, slots), 0) == iota((NGZ, slots), 1) // CAP
    cell_row = jnp.sum(jnp.where(mine, spread, 0.0), axis=0, keepdims=True)
    place = iota((192, slots), 0)
    slot = iota((192, slots), 1) // CAP
    group = jnp.where(slot >= LEFT, 2, jnp.where(slot >= RIGHT, 1, 0))
    inside = (lax.rem(place, 16) < ZL) & (place // 64 == group)
    target = jnp.where(inside, lax.rem(place, 64) // 16 * ZL + lax.rem(place, 16), -2)
    onehot = jnp.where(target.astype(F32) == cell_row, 1.0, 0.0).astype(BF16)
    r_hi, r_lo = split(wrecv[:, 0:CAP, :].reshape(slots, 128))
    wall = (dot(onehot, r_hi) + dot(onehot, r_lo)).reshape(3, XL, 16, 128)
    dsend[...] = wall[1:3, :, 0:ZL, :]
    sums = [
        remote(dsend.at[0], drecv.at[0], d_send.at[0], d_recv.at[0], gx, at(4, y)),
        remote(dsend.at[1], drecv.at[1], d_send.at[1], d_recv.at[1], gx, at(-4, y)),
    ]
    for c in sums:
        c.start()
    pl.semaphore_wait(known, 2)
    fields_at(NEAR + 1, 8, range(XL))
    for x in range(XL):
        send_field(8, x)
    loads[4].wait()
    m_hi, m_lo = split(m_f32[...])
    mh[...] = m_hi
    ml[...] = m_lo

    for c in sums:
        c.wait_recv()
    xsend[...] = wall[0, :, 0:ZL, :] + drecv[0] + drecv[1]
    for k in range(1, GY):
        other = lax.rem(y + k, GY)
        remote(
            xsend.at[other], xrecv.at[y], x_send.at[k - 1], x_recv.at[k - 1], gx, z * GY + other
        ).start()
    xrecv[y] = xsend[y]
    for k in range(1, GY):
        pltpu.make_async_copy(xsend.at[0], xrecv.at[0], x_recv.at[k - 1]).wait()
    given = jnp.concatenate([xrecv[...], jnp.zeros((GY, 16 - ZL, 128), F32)], axis=1)
    wall_t = jnp.transpose(given.reshape(64, 128))
    p = iota((64, 192), 0)
    col = iota((64, 192), 1)
    forcing = jnp.zeros((KW, 192), F32)
    for f in range(F):
        there = (lax.rem(p, 16) < ZL) & (col == WIN * f + ZL * (p // 16) + lax.rem(p, 16))
        there = jnp.where(there, 1.0, 0.0).astype(BF16)
        v_hi, v_lo = split(wall_t[KW * f : KW * (f + 1)])
        forcing = forcing + dot(v_hi, there) + dot(v_lo, there)

    pltpu.make_async_copy(fsend.at[others], frecv.at[others], f_recv).wait()
    left = frecv[:, 0:8, :].reshape(NY, 128)
    tail = frecv[:, 8:12, :]
    right = jnp.concatenate([tail[:, :, 0:64], tail[:, :, 64:128]], axis=1).reshape(NY, 64)
    columns = jnp.concatenate([left, right], axis=1)
    columns = jnp.concatenate([columns[0:KW] + forcing, columns[KW:]], axis=0)
    c_hi, c_lo = split(columns)
    solved = dot(mh[...], c_hi) + dot(mh[...], c_lo) + dot(ml[...], c_hi)
    bsend[:, 0:8, :] = solved[:, 0:128].reshape(NGZ, LEV, 128)
    back = solved[:, 128:192].reshape(NGZ, LEV, 64)
    bsend[:, 8:12, :] = jnp.concatenate([back[:, 0:4, :], back[:, 4:8, :]], axis=2)

    def send_back(i, c):
        d = lax.rem(me + i, NGZ)
        remote(bsend.at[d], brecv.at[me], b_send, b_recv, gx, d).start()
        return c

    lax.fori_loop(1, NGZ, send_back, 0)
    brecv[me] = bsend[me]
    pltpu.make_async_copy(bsend.at[others], brecv.at[others], b_recv).wait()

    for x in range(XL):
        pieces = [[] for _ in range(F)]
        for w in range(GZ):
            b0 = brecv[w * GY + x, 0:8, :]
            b1 = brecv[w * GY + x, 8:12, :]
            b1 = jnp.concatenate([b1[:, 0:64], b1[:, 64:128]], axis=0)
            pieces[0].append(b0[:, 0:48])
            pieces[1].append(b0[:, 48:96])
            pieces[2].append(b0[:, 96:128])
            pieces[2].append(b1[:, 0:16])
            pieces[3].append(b1[:, 16:64])
        for f in range(F):
            out_ref[f, x] = jnp.concatenate(pieces[f], axis=1)

    for h in halos:
        h.wait_send()
    pltpu.make_async_copy(wsend.at[got_wall], wrecv.at[got_wall], w_send).wait()
    for c in sums:
        c.wait_send()
    pltpu.make_async_copy(fsend.at[others], frecv.at[others], f_send).wait()
    pltpu.make_async_copy(bsend.at[others], brecv.at[others], b_send).wait()
    for k in range(1, GY):
        pltpu.make_async_copy(xsend.at[0], xrecv.at[0], x_send.at[k - 1]).wait()


def on_device(adjoint, velocity, shear, matrix, rows, cells, counts):
    anywhere = pl.BlockSpec(memory_space=pltpu.HBM)
    smem = pl.BlockSpec(memory_space=pltpu.SMEM)
    vmem = pltpu.VMEM
    dma = pltpu.SemaphoreType.DMA
    message = vmem((NGZ, ROWS, 128), F32)
    return pl.pallas_call(
        kernel,
        out_shape=jax.ShapeDtypeStruct((F, XL, LEV, NZ), F32),
        in_specs=[anywhere, smem, smem, anywhere, anywhere, anywhere, anywhere],
        out_specs=pl.BlockSpec(memory_space=pltpu.VMEM),
        scratch_shapes=[
            vmem((F, XL, LEV, NZ), F32),
            vmem((2, F, LEV, NZ), F32),
            vmem((NY, NY), F32),
            vmem((NY, NY), BF16),
            vmem((NY, NY), BF16),
            vmem((CAP, NGZ), jnp.int32),
            vmem((1, NGZ), jnp.int32),
            vmem((NGZ, CAP + 1, 128), F32),
            vmem((NGZ, CAP + 1, 128), F32),
            message, message, message, message,
            vmem((GY, ZL, 128), F32),
            vmem((GY, ZL, 128), F32),
            vmem((2, XL, ZL, 128), F32),
            vmem((2, XL, ZL, 128), F32),
            dma((5,)), dma((2,)), dma((2,)), dma, dma, dma, dma, dma, dma, dma((3,)), dma((3,)), dma((2,)), dma((2,)),
            pltpu.SemaphoreType.REGULAR,
        ],
        compiler_params=pltpu.CompilerParams(
            collective_id=0, has_side_effects=True, vmem_limit_bytes=64 * 1024 * 1024
        ),
        cost_estimate=pl.CostEstimate(flops=310_000_000, bytes_accessed=3_000_000, transcendentals=0),
    )(adjoint, velocity, shear, matrix, rows, jnp.swapaxes(cells, 2, 3), counts)


def solution(mesh):
    in_specs = (
        P(None, "gx", "gz", None),
        P("gz"),
        P("gz"),
        P(),
        P("gx", "gz", None, None, None),
        P("gx", "gz", None, None),
        P("gx", "gz", None),
    )
    return jax.shard_map(
        on_device, mesh=mesh, in_specs=in_specs, out_specs=P(None, "gx", "gz", None), check_vma=False
    )
```

```python
import functools

import jax
import jax.numpy as jnp
from jax import lax
from jax.experimental import pallas as pl
from jax.experimental.pallas import tpu as pltpu
from jax.sharding import PartitionSpec as P

MESH = pl.DeviceIdType.MESH
BF16 = jnp.bfloat16
F32 = jnp.float32

F, XL, NZ, NY = 4, 4, 768, 512
LEV = 8
NGX, NGZ, GY, GZ = 8, 64, 4, 16
WIN = NZ // GZ
ZL = 12
CAP = 8
KW = 32
NEAR = 4
DIRECT, RIGHT, LEFT = 0, 28, 46
ROWS = 12


def iota(shape, dim):
    return lax.broadcasted_iota(jnp.int32, shape, dim)


def split(x):
    hi = x.astype(BF16)
    return hi, (x - hi.astype(F32)).astype(BF16)


def dot(a, b):
    return jnp.dot(a, b, preferred_element_type=F32)


def pack(e, w):
    at = WIN * w
    first = jnp.concatenate(
        [e[0][:, at : at + 48], e[1][:, at : at + 48], e[2][:, at : at + 32]], axis=1
    )
    second = jnp.concatenate([e[2][:, at + 32 : at + 48], e[3][:, at : at + 48]], axis=1)
    return first, jnp.concatenate([second[0:4], second[4:8]], axis=1)


def kernel(
    adj_hbm, vel_ref, shear_ref, m_hbm, rows_hbm, cells_hbm, counts_hbm,
    out_ref,
    adj, halo, m_f32, mh, ml, cells, counts, wsend, wrecv, fsend, frecv, bsend, brecv, fsend2, frecv2, bsend2, brecv2, xsend, xrecv, dsend, drecv,
    local_sem, halo_send, halo_recv, w_send, w_recv, f_send, f_recv, b_send, b_recv, f_send2, f_recv2, b_send2, b_recv2, x_send, x_recv, d_send, d_recv, known,
):
    gx = lax.axis_index("gx")
    me = lax.axis_index("gz")
    z = me // GY
    y = lax.rem(me, GY)

    def remote(src, dst, ss, rs, ix, iz):
        return pltpu.make_async_remote_copy(
            src_ref=src, dst_ref=dst, send_sem=ss, recv_sem=rs, device_id=(ix, iz), device_id_type=MESH
        )

    def at(dz, iy):
        return lax.rem(z + dz + GZ, GZ) * GY + iy

    def signal(sem, ix, iz):
        pl.semaphore_signal(sem, inc=1, device_id=(ix, iz), device_id_type=MESH)

    barrier = pltpu.get_barrier_semaphore()
    after, before = lax.rem(gx + 1, NGX), lax.rem(gx + NGX - 1, NGX)
    signal(barrier, after, me)
    signal(barrier, before, me)

    def greet_here(k, c):
        signal(barrier, gx, at(0, lax.rem(y + k, GY)))
        return c

    def greet_near(k, c):
        signal(barrier, gx, at(NEAR - k // GY, lax.rem(k, GY)))
        signal(barrier, gx, at(k // GY - NEAR, lax.rem(k, GY)))
        return c

    lax.fori_loop(1, GY, greet_here, 0)
    lax.fori_loop(0, NEAR * GY, greet_near, 0)

    loads = [
        pltpu.make_async_copy(adj_hbm, adj, local_sem.at[0]),
        pltpu.make_async_copy(cells_hbm.at[0, 0], cells, local_sem.at[1]),
        pltpu.make_async_copy(counts_hbm.at[0], counts, local_sem.at[2]),
        pltpu.make_async_copy(rows_hbm.at[0, 0], wsend.at[:, pl.ds(0, CAP)], local_sem.at[3]),
        pltpu.make_async_copy(m_hbm, m_f32, local_sem.at[4]),
    ]
    for load in loads:
        load.start()

    loads[1].wait()
    loads[2].wait()
    used = iota((CAP, NGZ), 0) < counts[...]
    used_cells = jnp.where(used, cells[...], -1).astype(F32)
    used_cells = jnp.concatenate([used_cells, jnp.zeros((128 - CAP, NGZ), F32)], axis=0)
    loads[3].wait()
    wsend[:, CAP, :] = jnp.transpose(used_cells)

    level = iota((LEV, NZ), 0)
    velocity = jnp.zeros((LEV, NZ), F32)
    shear = jnp.zeros((LEV, NZ), F32)
    for i in range(LEV):
        velocity = jnp.where(level == i, vel_ref[i], velocity)
        shear = jnp.where(level == i, shear_ref[i], shear)

    def step_and_pack(x):
        rows = []
        for f in range(F):
            here = adj[f, x]
            up = adj[f, x + 1] if x < XL - 1 else halo[1, f]
            down = adj[f, x - 1] if x > 0 else halo[0, f]
            spanwise = pltpu.roll(here, NZ - 1, 1) + pltpu.roll(here, 1, 1) - 2.0 * here
            e = here + 0.5 * velocity * ((up - down) / 2.0) + 0.25 * spanwise
            if f == 1:
                e = e + 0.5 * shear * adj[0, x]
            rows.append(e)
        for w in range(GZ):
            first, second = pack(rows, w)
            fsend[w * GY + x] = first
            fsend2[w * GY + x] = second

    loads[0].wait()
    step_and_pack(1)
    step_and_pack(2)

    pl.semaphore_wait(barrier, 2 + (GY - 1) + 2 * NEAR * GY)
    signal(known, gx, at(NEAR, y))
    signal(known, gx, at(-NEAR, y))

    halos = [
        remote(adj.at[:, XL - 1], halo.at[0], halo_send.at[0], halo_recv.at[0], after, me),
        remote(adj.at[:, 0], halo.at[1], halo_send.at[1], halo_recv.at[1], before, me),
    ]
    for h in halos:
        h.start()

    def send_wall(owner_dz, dz, iy, slot):
        owner, dest = at(owner_dz, iy), at(dz, iy)
        remote(wsend.at[owner], wrecv.at[slot], w_send, w_recv, gx, dest).start()

    def send_first(dz, x):
        dest = at(dz, x)
        remote(fsend.at[dest], frecv.at[me], f_send, f_recv, gx, dest).start()

    def send_second(dz, x):
        dest = at(dz, x)
        remote(fsend2.at[dest], frecv2.at[me], f_send2, f_recv2, gx, dest).start()

    def wall_here(k, c):
        iy = lax.rem(y + k, GY)
        send_wall(0, 0, iy, DIRECT + 3 * GY + y)
        send_wall(4, 0, iy, RIGHT + y)
        send_wall(-4, 0, iy, LEFT + y)
        return c

    lax.fori_loop(1, GY, wall_here, 0)
    wrecv[DIRECT + 3 * GY + y] = wsend[me]
    wrecv[RIGHT + y] = wsend[at(4, y)]
    wrecv[LEFT + y] = wsend[at(-4, y)]

    def wall_at(level):
        def body(iy, c):
            send_wall(level, level, iy, DIRECT + (3 + level) * GY + y)
            send_wall(-level, -level, iy, DIRECT + (3 - level) * GY + y)
            send_wall(4 + level, level, iy, RIGHT + level * GY + y)
            send_wall(-4 - level, -level, iy, LEFT + level * GY + y)
            return c

        lax.fori_loop(0, GY, body, 0)

    for level in (1, 2, 3):
        wall_at(level)
    odd = lax.rem(y, 2)
    dz8 = NEAR - 2 * NEAR * odd
    slot8 = jnp.where(odd == 1, LEFT, RIGHT) + 4 * GY + y // 2

    def wall_8(iy, c):
        send_wall(8, dz8, iy, slot8)
        return c

    lax.fori_loop(0, GY, wall_8, 0)

    def fields_at(send, first, last, xs):
        def body(level, c):
            for x in xs:
                send(level, x)
                send(-level, x)
            return c

        lax.fori_loop(first, last, body, 0)

    def fields_here(send, xs):
        for x in xs:

            @pl.when(x != y)
            def _():
                send(0, x)

    fields_at(send_first, 1, NEAR + 1, (1, 2))
    fields_here(send_first, (1, 2))
    for h in halos:
        h.wait_recv()
    step_and_pack(0)
    step_and_pack(3)
    fields_at(send_first, 1, NEAR + 1, (0, 3))
    fields_here(send_first, (0, 3))
    frecv[me] = fsend[me]
    frecv2[me] = fsend2[me]

    others = pl.ds(0, NGZ - 1)
    got_wall = pl.ds(0, NGZ - 3)
    pltpu.make_async_copy(wsend.at[got_wall], wrecv.at[got_wall], w_recv).wait()
    slots = NGZ * CAP
    got = wrecv[:, CAP, :].astype(BF16)[:, 0:CAP]
    tile = (iota((CAP, slots), 0) == lax.rem(iota((CAP, slots), 1), CAP)).astype(BF16)
    spread = dot(got, tile)
    mine = iota((NGZ, slots), 0) == iota((NGZ, slots), 1) // CAP
    cell_row = jnp.sum(jnp.where(mine, spread, 0.0), axis=0, keepdims=True)
    place = iota((192, slots), 0)
    slot = iota((192, slots), 1) // CAP
    group = jnp.where(slot >= LEFT, 2, jnp.where(slot >= RIGHT, 1, 0))
    inside = (lax.rem(place, 16) < ZL) & (place // 64 == group)
    target = jnp.where(inside, lax.rem(place, 64) // 16 * ZL + lax.rem(place, 16), -2)
    onehot = jnp.where(target.astype(F32) == cell_row, 1.0, 0.0).astype(BF16)
    r_hi, r_lo = split(wrecv[:, 0:CAP, :].reshape(slots, 128))
    wall = (dot(onehot, r_hi) + dot(onehot, r_lo)).reshape(3, XL, 16, 128)
    dsend[...] = wall[1:3, :, 0:ZL, :]
    sums = [
        remote(dsend.at[0], drecv.at[0], d_send.at[0], d_recv.at[0], gx, at(4, y)),
        remote(dsend.at[1], drecv.at[1], d_send.at[1], d_recv.at[1], gx, at(-4, y)),
    ]
    for c in sums:
        c.start()
    pl.semaphore_wait(known, 2)
    fields_at(send_first, NEAR + 1, 8, range(XL))
    for x in range(XL):
        send_first(8, x)
    for x in range(XL):
        send_second(8, x)

    def second_at(k, c):
        for x in range(XL):
            send_second(8 - k, x)
            send_second(k - 8, x)
        return c

    lax.fori_loop(1, 8, second_at, 0)
    fields_here(send_second, range(XL))
    loads[4].wait()
    m_hi, m_lo = split(m_f32[...])
    mh[...] = m_hi
    ml[...] = m_lo

    for c in sums:
        c.wait_recv()
    xsend[...] = wall[0, :, 0:ZL, :] + drecv[0] + drecv[1]
    for k in range(1, GY):
        other = lax.rem(y + k, GY)
        remote(
            xsend.at[other], xrecv.at[y], x_send.at[k - 1], x_recv.at[k - 1], gx, z * GY + other
        ).start()
    xrecv[y] = xsend[y]
    for k in range(1, GY):
        pltpu.make_async_copy(xsend.at[0], xrecv.at[0], x_recv.at[k - 1]).wait()
    given = jnp.concatenate([xrecv[...], jnp.zeros((GY, 16 - ZL, 128), F32)], axis=1)
    wall_t = jnp.transpose(given.reshape(64, 128))
    p = iota((64, 192), 0)
    col = iota((64, 192), 1)
    forcing = jnp.zeros((KW, 192), F32)
    for f in range(F):
        there = (lax.rem(p, 16) < ZL) & (col == WIN * f + ZL * (p // 16) + lax.rem(p, 16))
        there = jnp.where(there, 1.0, 0.0).astype(BF16)
        v_hi, v_lo = split(wall_t[KW * f : KW * (f + 1)])
        forcing = forcing + dot(v_hi, there) + dot(v_lo, there)

    def product(columns, part):
        top = columns[0:KW] + forcing[:, part]
        c_hi, c_lo = split(jnp.concatenate([top, columns[KW:]], axis=0))
        return dot(mh[...], c_hi) + dot(mh[...], c_lo) + dot(ml[...], c_hi)

    def send_back(src, dst, ss, rs):
        def back(dest):
            remote(src.at[dest], dst.at[me], ss, rs, gx, dest).start()

        for iy in range(GY):
            back(at(8, iy))

        def body(k, c):
            for iy in range(GY):
                back(at(8 - k, iy))
                back(at(k - 8, iy))
            return c

        lax.fori_loop(1, 8, body, 0)
        for k in range(1, GY):
            back(at(0, lax.rem(y + k, GY)))
        dst[me] = src[me]

    pltpu.make_async_copy(fsend.at[others], frecv.at[others], f_recv).wait()
    left = product(frecv[...].reshape(NY, 128), slice(0, 128))
    bsend[...] = left.reshape(NGZ, LEV, 128)
    send_back(bsend, brecv, b_send, b_recv)

    pltpu.make_async_copy(fsend2.at[others], frecv2.at[others], f_recv2).wait()
    tail = frecv2[...]
    tail = jnp.concatenate([tail[:, :, 0:64], tail[:, :, 64:128]], axis=1)
    right = product(tail.reshape(NY, 64), slice(128, 192)).reshape(NGZ, LEV, 64)
    bsend2[...] = jnp.concatenate([right[:, 0:4, :], right[:, 4:8, :]], axis=2)
    send_back(bsend2, brecv2, b_send2, b_recv2)

    pltpu.make_async_copy(bsend.at[others], brecv.at[others], b_recv).wait()
    for x in range(XL):
        for f in range(2):
            out_ref[f, x] = jnp.concatenate(
                [brecv[w * GY + x, :, WIN * f : WIN * (f + 1)] for w in range(GZ)], axis=1
            )
    pltpu.make_async_copy(bsend2.at[others], brecv2.at[others], b_recv2).wait()
    for x in range(XL):
        pieces = [[], []]
        for w in range(GZ):
            b0 = brecv[w * GY + x]
            b1 = brecv2[w * GY + x]
            b1 = jnp.concatenate([b1[:, 0:64], b1[:, 64:128]], axis=0)
            pieces[0] += [b0[:, 96:128], b1[:, 0:16]]
            pieces[1].append(b1[:, 16:64])
        out_ref[2, x] = jnp.concatenate(pieces[0], axis=1)
        out_ref[3, x] = jnp.concatenate(pieces[1], axis=1)

    for h in halos:
        h.wait_send()
    pltpu.make_async_copy(wsend.at[got_wall], wrecv.at[got_wall], w_send).wait()
    for c in sums:
        c.wait_send()
    pltpu.make_async_copy(fsend.at[others], frecv.at[others], f_send).wait()
    pltpu.make_async_copy(bsend.at[others], brecv.at[others], b_send).wait()
    pltpu.make_async_copy(fsend2.at[others], frecv2.at[others], f_send2).wait()
    pltpu.make_async_copy(bsend2.at[others], brecv2.at[others], b_send2).wait()
    for k in range(1, GY):
        pltpu.make_async_copy(xsend.at[0], xrecv.at[0], x_send.at[k - 1]).wait()


def on_device(adjoint, velocity, shear, matrix, rows, cells, counts):
    anywhere = pl.BlockSpec(memory_space=pltpu.HBM)
    smem = pl.BlockSpec(memory_space=pltpu.SMEM)
    vmem = pltpu.VMEM
    dma = pltpu.SemaphoreType.DMA
    first, second = vmem((NGZ, 8, 128), F32), vmem((NGZ, 4, 128), F32)
    return pl.pallas_call(
        kernel,
        out_shape=jax.ShapeDtypeStruct((F, XL, LEV, NZ), F32),
        in_specs=[anywhere, smem, smem, anywhere, anywhere, anywhere, anywhere],
        out_specs=pl.BlockSpec(memory_space=pltpu.VMEM),
        scratch_shapes=[
            vmem((F, XL, LEV, NZ), F32),
            vmem((2, F, LEV, NZ), F32),
            vmem((NY, NY), F32),
            vmem((NY, NY), BF16),
            vmem((NY, NY), BF16),
            vmem((CAP, NGZ), jnp.int32),
            vmem((1, NGZ), jnp.int32),
            vmem((NGZ, CAP + 1, 128), F32),
            vmem((NGZ, CAP + 1, 128), F32),
            first, first, first, first, second, second, second, second,
            vmem((GY, ZL, 128), F32),
            vmem((GY, ZL, 128), F32),
            vmem((2, XL, ZL, 128), F32),
            vmem((2, XL, ZL, 128), F32),
            dma((5,)), dma((2,)), dma((2,)), *[dma] * 10, dma((3,)), dma((3,)), dma((2,)), dma((2,)),
            pltpu.SemaphoreType.REGULAR,
        ],
        compiler_params=pltpu.CompilerParams(
            collective_id=0, has_side_effects=True, vmem_limit_bytes=64 * 1024 * 1024
        ),
        cost_estimate=pl.CostEstimate(flops=310_000_000, bytes_accessed=3_000_000, transcendentals=0),
    )(adjoint, velocity, shear, matrix, rows, jnp.swapaxes(cells, 2, 3), counts)


def solution(mesh):
    in_specs = (
        P(None, "gx", "gz", None),
        P("gz"),
        P("gz"),
        P(),
        P("gx", "gz", None, None, None),
        P("gx", "gz", None, None),
        P("gx", "gz", None),
    )
    return jax.shard_map(
        on_device, mesh=mesh, in_specs=in_specs, out_specs=P(None, "gx", "gz", None), check_vma=False
    )
```

```python
import functools

import jax
import jax.numpy as jnp
from jax import lax
from jax.experimental import pallas as pl
from jax.experimental.pallas import tpu as pltpu
from jax.sharding import PartitionSpec as P

MESH = pl.DeviceIdType.MESH
BF16 = jnp.bfloat16
F32 = jnp.float32

F, XL, NZ, NY = 4, 4, 768, 512
LEV = 8
NGX, NGZ, GY, GZ = 8, 64, 4, 16
WIN = NZ // GZ
ZL = 12
CAP = 8
KW = 32
NEAR = 4
DIRECT, RIGHT, LEFT = 0, 28, 46


def iota(shape, dim):
    return lax.broadcasted_iota(jnp.int32, shape, dim)


def split(x):
    hi = x.astype(BF16)
    return hi, (x - hi.astype(F32)).astype(BF16)


def dot(a, b):
    return jnp.dot(a, b, preferred_element_type=F32)


def pack(e, w):
    at = WIN * w
    first = jnp.concatenate(
        [e[0][:, at : at + 48], e[1][:, at : at + 48], e[2][:, at : at + 32]], axis=1
    )
    second = jnp.concatenate([e[2][:, at + 32 : at + 48], e[3][:, at : at + 48]], axis=1)
    return first, jnp.concatenate([second[0:4], second[4:8]], axis=1)


def kernel(
    adj_hbm, vel_ref, shear_ref, m_hbm, rows_hbm, cells_hbm, counts_hbm,
    brecv, brecv2,
    adj, halo, m_f32, mh, ml, cells, counts, wsend, wrecv, fsend, frecv, bsend, fsend2, frecv2, bsend2, xsend, xrecv,
    local_sem, halo_send, halo_recv, w_send, w_recv, f_send, f_recv, b_send, b_recv, f_send2, f_recv2, b_send2, b_recv2, x_send, x_recv, known,
):
    gx = lax.axis_index("gx")
    me = lax.axis_index("gz")
    z = me // GY
    y = lax.rem(me, GY)

    def remote(src, dst, ss, rs, ix, iz):
        return pltpu.make_async_remote_copy(
            src_ref=src, dst_ref=dst, send_sem=ss, recv_sem=rs, device_id=(ix, iz), device_id_type=MESH
        )

    def at(dz, iy):
        return lax.rem(z + dz + GZ, GZ) * GY + iy

    def signal(sem, ix, iz):
        pl.semaphore_signal(sem, inc=1, device_id=(ix, iz), device_id_type=MESH)

    barrier = pltpu.get_barrier_semaphore()
    after, before = lax.rem(gx + 1, NGX), lax.rem(gx + NGX - 1, NGX)
    signal(barrier, after, me)
    signal(barrier, before, me)

    def greet_here(k, c):
        signal(barrier, gx, at(0, lax.rem(y + k, GY)))
        return c

    def greet_near(k, c):
        signal(barrier, gx, at(NEAR - k // GY, lax.rem(k, GY)))
        signal(barrier, gx, at(k // GY - NEAR, lax.rem(k, GY)))
        return c

    lax.fori_loop(1, GY, greet_here, 0)
    lax.fori_loop(0, NEAR * GY, greet_near, 0)

    loads = [
        pltpu.make_async_copy(adj_hbm, adj, local_sem.at[0]),
        pltpu.make_async_copy(cells_hbm.at[0, 0], cells, local_sem.at[1]),
        pltpu.make_async_copy(counts_hbm.at[0], counts, local_sem.at[2]),
        pltpu.make_async_copy(rows_hbm.at[0, 0], wsend.at[:, pl.ds(0, CAP)], local_sem.at[3]),
        pltpu.make_async_copy(m_hbm, m_f32, local_sem.at[4]),
    ]
    for load in loads:
        load.start()

    loads[1].wait()
    loads[2].wait()
    used = iota((CAP, NGZ), 0) < counts[...]
    used_cells = jnp.where(used, cells[...], -1).astype(F32)
    used_cells = jnp.concatenate([used_cells, jnp.zeros((128 - CAP, NGZ), F32)], axis=0)
    loads[3].wait()
    wsend[:, CAP, :] = jnp.transpose(used_cells)

    level = iota((LEV, NZ), 0)
    velocity = jnp.zeros((LEV, NZ), F32)
    shear = jnp.zeros((LEV, NZ), F32)
    for i in range(LEV):
        velocity = jnp.where(level == i, vel_ref[i], velocity)
        shear = jnp.where(level == i, shear_ref[i], shear)

    def step_and_pack(x):
        rows = []
        for f in range(F):
            here = adj[f, x]
            up = adj[f, x + 1] if x < XL - 1 else halo[1, f]
            down = adj[f, x - 1] if x > 0 else halo[0, f]
            spanwise = pltpu.roll(here, NZ - 1, 1) + pltpu.roll(here, 1, 1) - 2.0 * here
            e = here + 0.5 * velocity * ((up - down) / 2.0) + 0.25 * spanwise
            if f == 1:
                e = e + 0.5 * shear * adj[0, x]
            rows.append(e)
        for w in range(GZ):
            first, second = pack(rows, w)
            fsend[w * GY + x] = first
            fsend2[w * GY + x] = second

    loads[0].wait()
    step_and_pack(1)
    step_and_pack(2)

    pl.semaphore_wait(barrier, 2 + (GY - 1) + 2 * NEAR * GY)
    signal(known, gx, at(NEAR, y))
    signal(known, gx, at(-NEAR, y))

    halos = []
    for f in range(F):
        halos += [
            remote(adj.at[f, XL - 1], halo.at[0, f], halo_send.at[0], halo_recv.at[0], after, me),
            remote(adj.at[f, 0], halo.at[1, f], halo_send.at[1], halo_recv.at[1], before, me),
        ]
    for h in halos:
        h.start()

    def send_wall(owner_dz, dz, iy, slot):
        owner, dest = at(owner_dz, iy), at(dz, iy)
        remote(wsend.at[owner], wrecv.at[slot], w_send, w_recv, gx, dest).start()

    def send_first(dz, x):
        dest = at(dz, x)
        remote(fsend.at[dest], frecv.at[me], f_send, f_recv, gx, dest).start()

    def send_second(dz, x):
        dest = at(dz, x)
        remote(fsend2.at[dest], frecv2.at[me], f_send2, f_recv2, gx, dest).start()

    def wall_here(k, c):
        iy = lax.rem(y + k, GY)
        send_wall(0, 0, iy, DIRECT + 3 * GY + y)
        send_wall(4, 0, iy, RIGHT + y)
        send_wall(-4, 0, iy, LEFT + y)
        return c

    lax.fori_loop(1, GY, wall_here, 0)
    wrecv[DIRECT + 3 * GY + y] = wsend[me]
    wrecv[RIGHT + y] = wsend[at(4, y)]
    wrecv[LEFT + y] = wsend[at(-4, y)]

    def wall_at(level):
        def body(iy, c):
            send_wall(level, level, iy, DIRECT + (3 + level) * GY + y)
            send_wall(-level, -level, iy, DIRECT + (3 - level) * GY + y)
            send_wall(4 + level, level, iy, RIGHT + level * GY + y)
            send_wall(-4 - level, -level, iy, LEFT + level * GY + y)
            return c

        lax.fori_loop(0, GY, body, 0)

    for level in (1, 2, 3):
        wall_at(level)
    odd = lax.rem(y, 2)
    dz8 = NEAR - 2 * NEAR * odd
    slot8 = jnp.where(odd == 1, LEFT, RIGHT) + 4 * GY + y // 2

    def wall_8(iy, c):
        send_wall(8, dz8, iy, slot8)
        return c

    lax.fori_loop(0, GY, wall_8, 0)

    def fields_at(send, first, last, xs):
        def body(level, c):
            for x in xs:
                send(level, x)
                send(-level, x)
            return c

        lax.fori_loop(first, last, body, 0)

    def fields_here(send, xs):
        for x in xs:

            @pl.when(x != y)
            def _():
                send(0, x)

    fields_at(send_first, 1, NEAR + 1, (1, 2))
    fields_here(send_first, (1, 2))
    for k in range(2):
        pltpu.make_async_copy(halo.at[k], halo.at[k], halo_recv.at[k]).wait()
    step_and_pack(0)
    step_and_pack(3)
    fields_at(send_first, 1, NEAR + 1, (0, 3))
    fields_here(send_first, (0, 3))
    frecv[me] = fsend[me]
    frecv2[me] = fsend2[me]

    pl.semaphore_wait(known, 2)
    fields_at(send_first, NEAR + 1, 8, range(XL))
    for x in range(XL):
        send_first(8, x)
    others = pl.ds(0, NGZ - 1)
    got_wall = pl.ds(0, NGZ - 3)
    pltpu.make_async_copy(wsend.at[got_wall], wrecv.at[got_wall], w_recv).wait()
    slots = NGZ * CAP
    got = wrecv[:, CAP, :].astype(BF16)[:, 0:CAP]
    tile = (iota((CAP, slots), 0) == lax.rem(iota((CAP, slots), 1), CAP)).astype(BF16)
    spread = dot(got, tile)
    mine = iota((NGZ, slots), 0) == iota((NGZ, slots), 1) // CAP
    cell_row = jnp.sum(jnp.where(mine, spread, 0.0), axis=0, keepdims=True)
    place = iota((192, slots), 0)
    slot = iota((192, slots), 1) // CAP
    group = jnp.where(slot >= LEFT, 2, jnp.where(slot >= RIGHT, 1, 0))
    inside = (lax.rem(place, 16) < ZL) & (place // 64 == group)
    target = jnp.where(inside, lax.rem(place, 64) // 16 * ZL + lax.rem(place, 16), -2)
    onehot = jnp.where(target.astype(F32) == cell_row, 1.0, 0.0).astype(BF16)
    r_hi, r_lo = split(wrecv[:, 0:CAP, :].reshape(slots, 128))
    wall = (dot(onehot, r_hi) + dot(onehot, r_lo)).reshape(3 * XL, 16, 128)
    xsend[...] = wall[:, 0:ZL]

    def send_sums(xc, c):
        there = gx, at(4, xc)
        remote(xsend.at[4 + xc], xrecv.at[4 + y], x_send, x_recv, *there).start()
        there = gx, at(-4, xc)
        remote(xsend.at[8 + xc], xrecv.at[8 + y], x_send, x_recv, *there).start()

        @pl.when(xc != y)
        def _():
            remote(xsend.at[xc], xrecv.at[y], x_send, x_recv, gx, at(0, xc)).start()

        return c

    lax.fori_loop(0, XL, send_sums, 0)
    xrecv[y] = xsend[y]
    for x in range(XL):
        send_second(8, x)

    def second_at(k, c):
        for x in range(XL):
            send_second(8 - k, x)
            send_second(k - 8, x)
        return c

    lax.fori_loop(1, 8, second_at, 0)
    fields_here(send_second, range(XL))
    loads[4].wait()
    m_hi, m_lo = split(m_f32[...])
    mh[...] = m_hi
    ml[...] = m_lo

    eleven = pl.ds(0, 3 * XL - 1)
    pltpu.make_async_copy(xsend.at[eleven], xrecv.at[eleven], x_recv).wait()
    sums = xrecv[0:GY] + xrecv[GY : 2 * GY] + xrecv[2 * GY :]
    given = jnp.concatenate([sums, jnp.zeros((GY, 16 - ZL, 128), F32)], axis=1)
    wall_t = jnp.transpose(given.reshape(64, 128))
    p = iota((64, 192), 0)
    col = iota((64, 192), 1)
    forcing = jnp.zeros((KW, 192), F32)
    for f in range(F):
        there = (lax.rem(p, 16) < ZL) & (col == WIN * f + ZL * (p // 16) + lax.rem(p, 16))
        there = jnp.where(there, 1.0, 0.0).astype(BF16)
        v_hi, v_lo = split(wall_t[KW * f : KW * (f + 1)])
        forcing = forcing + dot(v_hi, there) + dot(v_lo, there)

    own = [
        pltpu.make_async_copy(bsend.at[me], brecv.at[me], local_sem.at[0]),
        pltpu.make_async_copy(bsend2.at[me], brecv2.at[me], local_sem.at[1]),
    ]
    def product(columns, part):
        top = columns[0:KW] + forcing[:, part]
        c_hi, c_lo = split(jnp.concatenate([top, columns[KW:]], axis=0))
        return dot(mh[...], c_hi) + dot(mh[...], c_lo) + dot(ml[...], c_hi)

    def send_back(src, dst, ss, rs):
        def back(dest):
            remote(src.at[dest], dst.at[me], ss, rs, gx, dest).start()

        for iy in range(GY):
            back(at(8, iy))

        def body(k, c):
            for iy in range(GY):
                back(at(8 - k, iy))
                back(at(k - 8, iy))
            return c

        lax.fori_loop(1, 8, body, 0)
        for k in range(1, GY):
            back(at(0, lax.rem(y + k, GY)))

    pltpu.make_async_copy(fsend.at[others], frecv.at[others], f_recv).wait()
    left = product(frecv[...].reshape(NY, 128), slice(0, 128))
    bsend[...] = left.reshape(NGZ, LEV, 128)
    send_back(bsend, brecv, b_send, b_recv)
    own[0].start()

    pltpu.make_async_copy(fsend2.at[others], frecv2.at[others], f_recv2).wait()
    tail = frecv2[...]
    tail = jnp.concatenate([tail[:, :, 0:64], tail[:, :, 64:128]], axis=1)
    right = product(tail.reshape(NY, 64), slice(128, 192)).reshape(NGZ, LEV, 64)
    bsend2[...] = jnp.concatenate([right[:, 0:4, :], right[:, 4:8, :]], axis=2)
    send_back(bsend2, brecv2, b_send2, b_recv2)
    own[1].start()

    pltpu.make_async_copy(bsend.at[others], brecv.at[others], b_recv).wait()
    pltpu.make_async_copy(bsend2.at[others], brecv2.at[others], b_recv2).wait()
    for c in own:
        c.wait()
    for k in range(2):
        pltpu.make_async_copy(halo.at[k], halo.at[k], halo_send.at[k]).wait()
    pltpu.make_async_copy(wsend.at[got_wall], wrecv.at[got_wall], w_send).wait()
    pltpu.make_async_copy(xsend.at[eleven], xrecv.at[eleven], x_send).wait()
    pltpu.make_async_copy(fsend.at[others], frecv.at[others], f_send).wait()
    pltpu.make_async_copy(bsend.at[others], brecv.at[others], b_send).wait()
    pltpu.make_async_copy(fsend2.at[others], frecv2.at[others], f_send2).wait()
    pltpu.make_async_copy(bsend2.at[others], brecv2.at[others], b_send2).wait()


def unpack(first, second, out, got, got2, done, in_sem, out_sem):
    loads = []
    for x in range(XL):
        loads.append(
            (
                pltpu.make_async_copy(first.at[:, x], got.at[x], in_sem.at[0, x]),
                pltpu.make_async_copy(second.at[:, x], got2.at[x], in_sem.at[1, x]),
            )
        )
        for load in loads[x]:
            load.start()
    stores = [pltpu.make_async_copy(done.at[:, x], out.at[:, x], out_sem.at[x]) for x in range(XL)]
    for x in range(XL):
        for load in loads[x]:
            load.wait()
        pieces = [[] for _ in range(F)]
        for w in range(GZ):
            b0 = got[x, w]
            b1 = got2[x, w]
            b1 = jnp.concatenate([b1[:, 0:64], b1[:, 64:128]], axis=0)
            pieces[0].append(b0[:, 0:48])
            pieces[1].append(b0[:, 48:96])
            pieces[2] += [b0[:, 96:128], b1[:, 0:16]]
            pieces[3].append(b1[:, 16:64])
        for f in range(F):
            done[f, x] = jnp.concatenate(pieces[f], axis=1)
        stores[x].start()
    for store in stores:
        store.wait()


def on_device(adjoint, velocity, shear, matrix, rows, cells, counts):
    anywhere = pl.BlockSpec(memory_space=pltpu.HBM)
    smem = pl.BlockSpec(memory_space=pltpu.SMEM)
    vmem = pltpu.VMEM
    dma = pltpu.SemaphoreType.DMA
    first, second = vmem((NGZ, 8, 128), F32), vmem((NGZ, 4, 128), F32)
    back = pl.pallas_call(
        kernel,
        out_shape=[jax.ShapeDtypeStruct((NGZ, r, 128), F32) for r in (8, 4)],
        in_specs=[anywhere, smem, smem, anywhere, anywhere, anywhere, anywhere],
        out_specs=[anywhere, anywhere],
        scratch_shapes=[
            vmem((F, XL, LEV, NZ), F32),
            vmem((2, F, LEV, NZ), F32),
            vmem((NY, NY), F32),
            vmem((NY, NY), BF16),
            vmem((NY, NY), BF16),
            vmem((CAP, NGZ), jnp.int32),
            vmem((1, NGZ), jnp.int32),
            vmem((NGZ, CAP + 1, 128), F32),
            vmem((NGZ, CAP + 1, 128), F32),
            first, first, first, second, second, second,
            vmem((3 * XL, ZL, 128), F32),
            vmem((3 * GY, ZL, 128), F32),
            dma((5,)), dma((2,)), dma((2,)), *[dma] * 12,
            pltpu.SemaphoreType.REGULAR,
        ],
        compiler_params=pltpu.CompilerParams(
            collective_id=0, has_side_effects=True, vmem_limit_bytes=64 * 1024 * 1024
        ),
        cost_estimate=pl.CostEstimate(flops=310_000_000, bytes_accessed=3_000_000, transcendentals=0),
    )(adjoint, velocity, shear, matrix, rows, jnp.swapaxes(cells, 2, 3), counts)

    return pl.pallas_call(
        unpack,
        out_shape=jax.ShapeDtypeStruct((F, XL, LEV, NZ), F32),
        in_specs=[anywhere, anywhere],
        out_specs=anywhere,
        scratch_shapes=[
            vmem((XL, GZ, 8, 128), F32),
            vmem((XL, GZ, 4, 128), F32),
            vmem((F, XL, LEV, NZ), F32),
            dma((2, XL)),
            dma((XL,)),
        ],
        compiler_params=pltpu.CompilerParams(vmem_limit_bytes=64 * 1024 * 1024),
    )(*(b.reshape(GZ, GY, b.shape[1], 128) for b in back))


def solution(mesh):
    in_specs = (
        P(None, "gx", "gz", None),
        P("gz"),
        P("gz"),
        P(),
        P("gx", "gz", None, None, None),
        P("gx", "gz", None, None),
        P("gx", "gz", None),
    )
    return jax.shard_map(
        on_device, mesh=mesh, in_specs=in_specs, out_specs=P(None, "gx", "gz", None), check_vma=False
    )
```

```python
import functools

import jax
import jax.numpy as jnp
from jax import lax
from jax.experimental import pallas as pl
from jax.experimental.pallas import tpu as pltpu
from jax.sharding import PartitionSpec as P

MESH = pl.DeviceIdType.MESH
BF16 = jnp.bfloat16
F32 = jnp.float32

F, XL, NZ, NY = 4, 4, 768, 512
LEV = 8
NGX, NGZ, GY, GZ = 8, 64, 4, 16
WIN = NZ // GZ
ZL = 12
CAP = 8
KW = 32
NEAR = 4
DIRECT, RIGHT, LEFT = 0, 28, 46


def iota(shape, dim):
    return lax.broadcasted_iota(jnp.int32, shape, dim)


def split(x):
    hi = x.astype(BF16)
    return hi, (x - hi.astype(F32)).astype(BF16)


def dot(a, b):
    return jnp.dot(a, b, preferred_element_type=F32)


def pack(e, w):
    at = WIN * w
    first = jnp.concatenate(
        [e[0][:, at : at + 48], e[1][:, at : at + 48], e[2][:, at : at + 32]], axis=1
    )
    second = jnp.concatenate([e[2][:, at + 32 : at + 48], e[3][:, at : at + 48]], axis=1)
    return first, jnp.concatenate([second[0:4], second[4:8]], axis=1)


def kernel(
    adj_hbm, vel_ref, shear_ref, m_hbm, rows_hbm, cells_hbm, counts_hbm,
    brecv, brecv2,
    adj, halo, m_f32, mh, ml, cells, counts, wsend, wrecv, fsend, frecv, bsend, fsend2, frecv2, bsend2, xsend, xrecv,
    local_sem, halo_send, halo_recv, w_send, w_recv, s_recv, f_send, f_recv, b_send, b_recv, f_send2, f_recv2, b_send2, b_recv2, x_send, x_recv, known,
):
    gx = lax.axis_index("gx")
    me = lax.axis_index("gz")
    z = me // GY
    y = lax.rem(me, GY)

    def remote(src, dst, ss, rs, ix, iz):
        return pltpu.make_async_remote_copy(
            src_ref=src, dst_ref=dst, send_sem=ss, recv_sem=rs, device_id=(ix, iz), device_id_type=MESH
        )

    def at(dz, iy):
        return lax.rem(z + dz + GZ, GZ) * GY + iy

    def signal(sem, ix, iz):
        pl.semaphore_signal(sem, inc=1, device_id=(ix, iz), device_id_type=MESH)

    loads = [
        pltpu.make_async_copy(adj_hbm, adj, local_sem.at[0]),
        pltpu.make_async_copy(cells_hbm.at[0, 0], cells, local_sem.at[1]),
        pltpu.make_async_copy(counts_hbm.at[0], counts, local_sem.at[2]),
        pltpu.make_async_copy(rows_hbm.at[0, 0], wsend.at[:, pl.ds(0, CAP)], local_sem.at[3]),
        pltpu.make_async_copy(m_hbm, m_f32, local_sem.at[4]),
    ]
    for load in loads:
        load.start()

    barrier = pltpu.get_barrier_semaphore()
    after, before = lax.rem(gx + 1, NGX), lax.rem(gx + NGX - 1, NGX)
    signal(barrier, after, me)
    signal(barrier, before, me)

    def greet_here(k, c):
        signal(barrier, gx, at(0, lax.rem(y + k, GY)))
        return c

    def greet_near(k, c):
        signal(barrier, gx, at(NEAR - k // GY, lax.rem(k, GY)))
        signal(barrier, gx, at(k // GY - NEAR, lax.rem(k, GY)))
        return c

    lax.fori_loop(1, GY, greet_here, 0)
    lax.fori_loop(0, NEAR * GY, greet_near, 0)


    loads[1].wait()
    loads[2].wait()
    used = iota((CAP, NGZ), 0) < counts[...]
    used_cells = jnp.where(used, cells[...], -1).astype(F32)
    used_cells = jnp.concatenate([used_cells, jnp.zeros((128 - CAP, NGZ), F32)], axis=0)
    loads[3].wait()
    wsend[:, CAP, :] = jnp.transpose(used_cells)

    level = iota((LEV, NZ), 0)
    velocity = jnp.zeros((LEV, NZ), F32)
    shear = jnp.zeros((LEV, NZ), F32)
    for i in range(LEV):
        velocity = jnp.where(level == i, vel_ref[i], velocity)
        shear = jnp.where(level == i, shear_ref[i], shear)

    def step_and_pack(x):
        rows = []
        for f in range(F):
            here = adj[f, x]
            up = adj[f, x + 1] if x < XL - 1 else halo[1, f]
            down = adj[f, x - 1] if x > 0 else halo[0, f]
            spanwise = pltpu.roll(here, NZ - 1, 1) + pltpu.roll(here, 1, 1) - 2.0 * here
            e = here + 0.5 * velocity * ((up - down) / 2.0) + 0.25 * spanwise
            if f == 1:
                e = e + 0.5 * shear * adj[0, x]
            rows.append(e)
        for w in range(GZ):
            first, second = pack(rows, w)
            fsend[w * GY + x] = first
            fsend2[w * GY + x] = second

    loads[0].wait()
    step_and_pack(1)
    step_and_pack(2)

    pl.semaphore_wait(barrier, 2 + (GY - 1) + 2 * NEAR * GY)
    signal(known, gx, at(NEAR, y))
    signal(known, gx, at(-NEAR, y))

    halos = []
    for f in range(F):
        halos += [
            remote(adj.at[f, XL - 1], halo.at[0, f], halo_send.at[0], halo_recv.at[0], after, me),
            remote(adj.at[f, 0], halo.at[1, f], halo_send.at[1], halo_recv.at[1], before, me),
        ]
    for h in halos:
        h.start()

    def send_wall(owner_dz, dz, iy, slot, arrived):
        owner, dest = at(owner_dz, iy), at(dz, iy)
        remote(wsend.at[owner], wrecv.at[slot], w_send, arrived, gx, dest).start()

    def send_first(dz, x):
        dest = at(dz, x)
        remote(fsend.at[dest], frecv.at[me], f_send, f_recv, gx, dest).start()

    def send_second(dz, x):
        dest = at(dz, x)
        remote(fsend2.at[dest], frecv2.at[me], f_send2, f_recv2, gx, dest).start()

    odd = lax.rem(y, 2)
    dz8 = NEAR - 2 * NEAR * odd
    slot8 = jnp.where(odd == 1, LEFT, RIGHT) + 4 * GY + y // 2

    def wall_8(iy, c):
        send_wall(8, dz8, iy, slot8, s_recv)
        return c

    def wall_summed(k, c):
        level, iy = 3 - k // GY, lax.rem(k, GY)
        send_wall(4 + level, level, iy, RIGHT + level * GY + y, s_recv)
        send_wall(-4 - level, -level, iy, LEFT + level * GY + y, s_recv)
        return c

    def wall_summed_here(k, c):
        iy = lax.rem(y + k, GY)
        send_wall(4, 0, iy, RIGHT + y, s_recv)
        send_wall(-4, 0, iy, LEFT + y, s_recv)
        return c

    def wall_direct(k, c):
        level, iy = 3 - k // GY, lax.rem(k, GY)
        send_wall(level, level, iy, DIRECT + (3 + level) * GY + y, w_recv)
        send_wall(-level, -level, iy, DIRECT + (3 - level) * GY + y, w_recv)
        return c

    def wall_direct_here(k, c):
        send_wall(0, 0, lax.rem(y + k, GY), DIRECT + 3 * GY + y, w_recv)
        return c

    lax.fori_loop(0, GY, wall_8, 0)
    lax.fori_loop(0, 3 * GY, wall_summed, 0)
    lax.fori_loop(1, GY, wall_summed_here, 0)
    lax.fori_loop(0, 3 * GY, wall_direct, 0)
    lax.fori_loop(1, GY, wall_direct_here, 0)
    wrecv[DIRECT + 3 * GY + y] = wsend[me]
    wrecv[RIGHT + y] = wsend[at(4, y)]
    wrecv[LEFT + y] = wsend[at(-4, y)]

    def fields_at(send, first, last, xs):
        def body(level, c):
            for x in xs:
                send(level, x)
                send(-level, x)
            return c

        lax.fori_loop(first, last, body, 0)

    def fields_here(send, xs):
        for x in xs:

            @pl.when(x != y)
            def _():
                send(0, x)

    fields_at(send_first, 1, NEAR + 1, (1, 2))
    fields_here(send_first, (1, 2))
    for k in range(2):
        pltpu.make_async_copy(halo.at[k], halo.at[k], halo_recv.at[k]).wait()
    step_and_pack(0)
    step_and_pack(3)
    fields_at(send_first, 1, NEAR + 1, (0, 3))
    fields_here(send_first, (0, 3))
    frecv[me] = fsend[me]
    frecv2[me] = fsend2[me]

    others = pl.ds(0, NGZ - 1)

    def sums(first, last, groups):
        slots = (last - first) * CAP
        got = wrecv[first:last, CAP, :].astype(BF16)[:, 0:CAP]
        tile = (iota((CAP, slots), 0) == lax.rem(iota((CAP, slots), 1), CAP)).astype(BF16)
        spread = dot(got, tile)
        mine = iota((last - first, slots), 0) == iota((last - first, slots), 1) // CAP
        cell_row = jnp.sum(jnp.where(mine, spread, 0.0), axis=0, keepdims=True)
        place = iota((groups * 64, slots), 0)
        group = iota((groups * 64, slots), 1) // (slots // groups)
        inside = (lax.rem(place, 16) < ZL) & (place // 64 == group)
        target = jnp.where(inside, lax.rem(place, 64) // 16 * ZL + lax.rem(place, 16), -2)
        onehot = jnp.where(target.astype(F32) == cell_row, 1.0, 0.0).astype(BF16)
        r_hi, r_lo = split(wrecv[first:last, 0:CAP, :].reshape(slots, 128))
        wall = dot(onehot, r_hi) + dot(onehot, r_lo)
        return wall.reshape(groups * XL, 16, 128)[:, 0:ZL]

    def send_far_sums(xc, c):
        there = gx, at(4, xc)
        remote(xsend.at[4 + xc], xrecv.at[4 + y], x_send, x_recv, *there).start()
        there = gx, at(-4, xc)
        remote(xsend.at[8 + xc], xrecv.at[8 + y], x_send, x_recv, *there).start()
        return c

    def send_near_sums(k, c):
        xc = lax.rem(y + k, XL)
        remote(xsend.at[xc], xrecv.at[y], x_send, x_recv, gx, at(0, xc)).start()
        return c

    pl.semaphore_wait(known, 2)
    fields_at(send_first, NEAR + 1, 8, range(XL))
    for x in range(XL):
        send_first(8, x)
    summed = pl.ds(0, NGZ - RIGHT - 2)
    pltpu.make_async_copy(wsend.at[summed], wrecv.at[summed], s_recv).wait()
    xsend[XL:] = sums(RIGHT, NGZ, 2)
    lax.fori_loop(0, XL, send_far_sums, 0)


    direct = pl.ds(0, RIGHT - 1)
    pltpu.make_async_copy(wsend.at[direct], wrecv.at[direct], w_recv).wait()
    xsend[0:XL] = sums(DIRECT, RIGHT, 1)
    lax.fori_loop(1, XL, send_near_sums, 0)
    xrecv[y] = xsend[y]
    for x in range(XL):
        send_second(8, x)

    def second_at(k, c):
        for x in range(XL):
            send_second(8 - k, x)
            send_second(k - 8, x)
        return c

    lax.fori_loop(1, 8, second_at, 0)
    fields_here(send_second, range(XL))
    loads[4].wait()
    m_hi, m_lo = split(m_f32[...])
    mh[...] = m_hi
    ml[...] = m_lo

    eleven = pl.ds(0, 3 * XL - 1)
    pltpu.make_async_copy(xsend.at[eleven], xrecv.at[eleven], x_recv).wait()
    given = jnp.concatenate([xrecv[0:GY] + xrecv[GY : 2 * GY] + xrecv[2 * GY :], jnp.zeros((GY, 16 - ZL, 128), F32)], axis=1)
    wall_t = jnp.transpose(given.reshape(64, 128))
    p = iota((64, 192), 0)
    col = iota((64, 192), 1)
    forcing = jnp.zeros((KW, 192), F32)
    for f in range(F):
        there = (lax.rem(p, 16) < ZL) & (col == WIN * f + ZL * (p // 16) + lax.rem(p, 16))
        there = jnp.where(there, 1.0, 0.0).astype(BF16)
        v_hi, v_lo = split(wall_t[KW * f : KW * (f + 1)])
        forcing = forcing + dot(v_hi, there) + dot(v_lo, there)

    own = [
        pltpu.make_async_copy(bsend.at[me], brecv.at[me], local_sem.at[0]),
        pltpu.make_async_copy(bsend2.at[me], brecv2.at[me], local_sem.at[1]),
    ]
    def product(columns, part):
        top = columns[0:KW] + forcing[:, part]
        c_hi, c_lo = split(jnp.concatenate([top, columns[KW:]], axis=0))
        return dot(mh[...], c_hi) + dot(mh[...], c_lo) + dot(ml[...], c_hi)

    def send_back(src, dst, ss, rs):
        def back(dest):
            remote(src.at[dest], dst.at[me], ss, rs, gx, dest).start()

        for iy in range(GY):
            back(at(8, iy))

        def body(k, c):
            for iy in range(GY):
                back(at(8 - k, iy))
                back(at(k - 8, iy))
            return c

        lax.fori_loop(1, 8, body, 0)
        for k in range(1, GY):
            back(at(0, lax.rem(y + k, GY)))

    pltpu.make_async_copy(fsend.at[others], frecv.at[others], f_recv).wait()
    left = product(frecv[...].reshape(NY, 128), slice(0, 128))
    bsend[...] = left.reshape(NGZ, LEV, 128)
    send_back(bsend, brecv, b_send, b_recv)
    own[0].start()

    pltpu.make_async_copy(fsend2.at[others], frecv2.at[others], f_recv2).wait()
    tail = frecv2[...]
    tail = jnp.concatenate([tail[:, :, 0:64], tail[:, :, 64:128]], axis=1)
    right = product(tail.reshape(NY, 64), slice(128, 192)).reshape(NGZ, LEV, 64)
    bsend2[...] = jnp.concatenate([right[:, 0:4, :], right[:, 4:8, :]], axis=2)
    send_back(bsend2, brecv2, b_send2, b_recv2)
    own[1].start()

    pltpu.make_async_copy(bsend.at[others], brecv.at[others], b_recv).wait()
    pltpu.make_async_copy(bsend2.at[others], brecv2.at[others], b_recv2).wait()
    for c in own:
        c.wait()
    for k in range(2):
        pltpu.make_async_copy(halo.at[k], halo.at[k], halo_send.at[k]).wait()
    sent = pl.ds(0, NGZ - 3)
    pltpu.make_async_copy(wsend.at[sent], wrecv.at[sent], w_send).wait()
    pltpu.make_async_copy(xsend.at[eleven], xrecv.at[eleven], x_send).wait()
    pltpu.make_async_copy(fsend.at[others], frecv.at[others], f_send).wait()
    pltpu.make_async_copy(bsend.at[others], brecv.at[others], b_send).wait()
    pltpu.make_async_copy(fsend2.at[others], frecv2.at[others], f_send2).wait()
    pltpu.make_async_copy(bsend2.at[others], brecv2.at[others], b_send2).wait()


def unpack(first, second, out, got, got2, done, in_sem, out_sem):
    loads = []
    for x in range(XL):
        loads.append(
            (
                pltpu.make_async_copy(first.at[:, x], got.at[x], in_sem.at[0, x]),
                pltpu.make_async_copy(second.at[:, x], got2.at[x], in_sem.at[1, x]),
            )
        )
        for load in loads[x]:
            load.start()
    stores = [pltpu.make_async_copy(done.at[:, x], out.at[:, x], out_sem.at[x]) for x in range(XL)]
    for x in range(XL):
        for load in loads[x]:
            load.wait()
        pieces = [[] for _ in range(F)]
        for w in range(GZ):
            b0 = got[x, w]
            b1 = got2[x, w]
            b1 = jnp.concatenate([b1[:, 0:64], b1[:, 64:128]], axis=0)
            pieces[0].append(b0[:, 0:48])
            pieces[1].append(b0[:, 48:96])
            pieces[2] += [b0[:, 96:128], b1[:, 0:16]]
            pieces[3].append(b1[:, 16:64])
        for f in range(F):
            done[f, x] = jnp.concatenate(pieces[f], axis=1)
        stores[x].start()
    for store in stores:
        store.wait()


def on_device(adjoint, velocity, shear, matrix, rows, cells, counts):
    anywhere = pl.BlockSpec(memory_space=pltpu.HBM)
    smem = pl.BlockSpec(memory_space=pltpu.SMEM)
    vmem = pltpu.VMEM
    dma = pltpu.SemaphoreType.DMA
    first, second = vmem((NGZ, 8, 128), F32), vmem((NGZ, 4, 128), F32)
    back = pl.pallas_call(
        kernel,
        out_shape=[jax.ShapeDtypeStruct((NGZ, r, 128), F32) for r in (8, 4)],
        in_specs=[anywhere, smem, smem, anywhere, anywhere, anywhere, anywhere],
        out_specs=[anywhere, anywhere],
        scratch_shapes=[
            vmem((F, XL, LEV, NZ), F32),
            vmem((2, F, LEV, NZ), F32),
            vmem((NY, NY), F32),
            vmem((NY, NY), BF16),
            vmem((NY, NY), BF16),
            vmem((CAP, NGZ), jnp.int32),
            vmem((1, NGZ), jnp.int32),
            vmem((NGZ, CAP + 1, 128), F32),
            vmem((NGZ, CAP + 1, 128), F32),
            first, first, first, second, second, second,
            vmem((3 * XL, ZL, 128), F32),
            vmem((3 * GY, ZL, 128), F32),
            dma((5,)), dma((2,)), dma((2,)), *[dma] * 13,
            pltpu.SemaphoreType.REGULAR,
        ],
        compiler_params=pltpu.CompilerParams(
            collective_id=0, has_side_effects=True, vmem_limit_bytes=64 * 1024 * 1024
        ),
        cost_estimate=pl.CostEstimate(flops=310_000_000, bytes_accessed=3_000_000, transcendentals=0),
    )(adjoint, velocity, shear, matrix, rows, jnp.swapaxes(cells, 2, 3), counts)

    return pl.pallas_call(
        unpack,
        out_shape=jax.ShapeDtypeStruct((F, XL, LEV, NZ), F32),
        in_specs=[anywhere, anywhere],
        out_specs=anywhere,
        scratch_shapes=[
            vmem((XL, GZ, 8, 128), F32),
            vmem((XL, GZ, 4, 128), F32),
            vmem((F, XL, LEV, NZ), F32),
            dma((2, XL)),
            dma((XL,)),
        ],
        compiler_params=pltpu.CompilerParams(vmem_limit_bytes=64 * 1024 * 1024),
    )(*(b.reshape(GZ, GY, b.shape[1], 128) for b in back))


def solution(mesh):
    in_specs = (
        P(None, "gx", "gz", None),
        P("gz"),
        P("gz"),
        P(),
        P("gx", "gz", None, None, None),
        P("gx", "gz", None, None),
        P("gx", "gz", None),
    )
    return jax.shard_map(
        on_device, mesh=mesh, in_specs=in_specs, out_specs=P(None, "gx", "gz", None), check_vma=False
    )
```
